32 devices in a mesh: dp: 16 (over z, x, core), tensor: 2 (over y).
Axes of the slice: x: 2, y: 2, z: 4, core: 2. Of those that a mesh axis runs over, the one named last changes fastest.
Arguments:
- activations: bfloat16 [12288, 4096], P('dp'), may hold values from -6 to 6
- grad_out: bfloat16 [12288, 2, 1024], P('dp', None, 'tensor'), may hold values from -0.059814453 to 0.059814453
- weights: float32 [4096, 2, 1024], P('dp', None, 'tensor')
- first_moment: float32 [4096, 2, 1024], P('dp', None, 'tensor'), may hold values from -6 to 6
- second_moment: float32 [4096, 2, 1024], P('dp', None, 'tensor')
- step: int32 [1], replicated, may hold values from 1 to 40
Outputs:
- new_weights: float32 [4096, 2, 1024], P('dp', None, 'tensor')
- new_first: float32 [4096, 2, 1024], P('dp', None, 'tensor')
- new_second: float32 [4096, 2, 1024], P('dp', None, 'tensor')
- ratios: float32 [2], replicated
- new_kv: bfloat16 [12288, 2, 1024], P('dp', None, 'tensor')
The draws below stay inside these ranges and needn't reach their ends.
All inputs are finite; a program needn't handle non-finite values.
Results may differ from the reference program's by a relative error of at most 0.001.
The reference program's roundings to bfloat16 on the way (of `half_weights`) count: a program that leaves them out, or rounds other values in their place, can miss the bound.
Values may be sent and summed in bfloat16 or wider, within the bound.
No kernel may reach another device: no remote copies, remote signals or barrier semaphores. Data moves between devices by JAX's collectives and lax.ppermute only.
A program may use at most 64 MiB of HBM per device.

```python
import math
import jax
import jax.numpy as jnp
from jax import lax

D = 4096
KVW = 1024
TOKENS = 12288


def factor_line(key, count, rise):
    spread = jax.random.uniform(key, (count,), jnp.float32)
    place = jnp.arange(count, dtype=jnp.float32) / (count - 1)
    return jnp.power(10.0, spread - 0.5) * jnp.power(rise, place - 0.5)


def draw_weights(key, part):
    rise = 1.7320508
    base = jax.random.normal(jax.random.fold_in(key, 11), (D, 2, KVW), jnp.float32)
    row_scale = factor_line(jax.random.fold_in(key, 12), D, rise)
    col_scale = factor_line(jax.random.fold_in(key, 13), KVW, rise)
    return base * row_scale[:, None, None] * col_scale[None, None, :]


def draw_second_moment(key, part):
    rise = 3.0
    base = jax.random.uniform(jax.random.fold_in(key, 21), (D, 2, KVW), jnp.float32, 0.5, 2.0)
    row_scale = factor_line(jax.random.fold_in(key, 22), D, rise)
    col_scale = factor_line(jax.random.fold_in(key, 23), KVW, rise)
    return 0.5 * base / (row_scale[:, None, None] * col_scale[None, None, :])


def with_spikes(drawn, own_key, source, target, parts, factor):
    owner, partner = [(jnp.arange(drawn.shape[dim]) // (drawn.shape[dim] // parts)).reshape([-1 if axis == dim else 1 for axis in range(drawn.ndim)]) for dim in (source, target)]
    chosen = jax.random.permutation(own_key, parts)[partner]
    strong = (owner == chosen) | (owner == (partner + parts // 2) % parts)
    return jnp.where(strong, factor * drawn, drawn)


def steps_of(stream_key, shape, pieces, low, largest):
    def one(axis_at, parts):
        heights = jax.random.uniform(jax.random.fold_in(jax.random.fold_in(stream_key, 6), axis_at), (parts,), jnp.float32, low / len(pieces), largest / len(pieces))
        return jnp.repeat(jnp.exp(heights), shape[axis_at] // parts).reshape((-1,) + (1,) * (len(shape) - axis_at - 1))

    loudness = one(*pieces[0])
    for cut in pieces[1:]:
        loudness = loudness * one(*cut)
    return loudness


def noise(own_key, dims, scale, most, split=(), kind=jnp.bfloat16):
    factor_of = steps_of(own_key, dims, split, -0.22, 0.18) if split else 1.0
    array = jax.random.normal(own_key, dims, jnp.float32) * scale * factor_of
    return jnp.minimum(jnp.maximum(array, -most), most).astype(kind)


def noise_with(rng, shape, width, reach, split, heavy, kind=jnp.bfloat16):
    entries = width * jax.random.normal(rng, shape, jnp.float32)
    if split:
        entries = entries * steps_of(rng, shape, split, -0.22, 0.18)
    return jnp.clip(with_spikes(entries, jax.random.fold_in(rng, 3), *heavy), -reach, reach).astype(kind)


def setup_inputs(seed: int = 0) -> dict:
    splits = jax.random.split(jax.random.key(seed), 7)
    return {
        "activations": noise_with(splits[0], (TOKENS, D), 1.0, 6.0, ((0, 16),), (0, 1, 16, 2.0)),
        "grad_out": noise(splits[1], (TOKENS, 2, KVW), 0.01, 0.059814453, ((0, 16), (2, 2))),
        "weights": draw_weights(jax.random.fold_in(splits[6], 71), 0),
        "first_moment": noise(splits[3], (D, 2, KVW), 1.0, 6.0, ((0, 16), (2, 2)), jnp.float32),
        "second_moment": draw_second_moment(jax.random.fold_in(splits[6], 71), 0),
        "step": jax.random.randint(splits[5], (1,), 1, 41).astype(jnp.int32),
    }


def reference(activations, grad_out, weights, first_moment, second_moment, step):
    inputs = activations.astype(jnp.float32)
    grad = jnp.einsum('td,tsc->dsc', inputs, grad_out.astype(jnp.float32))
    new_first = 0.9 * first_moment + 0.1 * grad
    new_second = 0.95 * second_moment + 0.05 * grad * grad
    count = step[0].astype(jnp.float32)
    bias_one = 1.0 - jnp.exp(count * math.log(0.9))
    bias_two = 1.0 - jnp.exp(count * math.log(0.95))
    update = new_first / bias_one / (jnp.sqrt(new_second / bias_two) + 1e-06) + 0.1 * weights
    weight_sq = lax.optimization_barrier(jnp.sum(weights * weights, axis=(0, 2)))
    update_sq = lax.optimization_barrier(jnp.sum(update * update, axis=(0, 2)))
    ratios = jnp.sqrt(weight_sq) / (jnp.sqrt(update_sq) + 1e-06)
    new_weights = weights - 0.05 * ratios[None, :, None] * update
    half_weights = new_weights.astype(jnp.bfloat16)
    new_kv = jnp.einsum('td,dsc->tsc', inputs, half_weights.astype(jnp.float32)).astype(jnp.bfloat16)
    return (new_weights, new_first, new_second, ratios, new_kv)
```

```python
import math

import jax
import jax.numpy as jnp
from jax import lax
from jax.experimental import pallas as pl
from jax.experimental.pallas import tpu as pltpu
from jax.sharding import PartitionSpec as P

F32 = jnp.float32
LANES = 128


def after(value, *others):
    return lax.optimization_barrier((value, *others))[0]


def pick_blocks(activations, blocks, width):
    if width % LANES:
        return jnp.concatenate(
            [lax.dynamic_slice_in_dim(activations, block * width, width, 1) for block in blocks], axis=1
        )
    count = len(blocks)

    def kernel(places, src, dst, sems):
        copies = [
            pltpu.make_async_copy(
                src.at[:, pl.ds(pl.multiple_of(places[i] * width, width), width)],
                dst.at[:, pl.ds(i * width, width)],
                sems.at[i],
            )
            for i in range(count)
        ]
        for copy in copies:
            copy.start()
        for copy in copies:
            copy.wait()

    return pl.pallas_call(
        kernel,
        out_shape=jax.ShapeDtypeStruct((activations.shape[0], count * width), activations.dtype),
        in_specs=[pl.BlockSpec(memory_space=pltpu.SMEM), pl.BlockSpec(memory_space=pl.ANY)],
        out_specs=pl.BlockSpec(memory_space=pltpu.VMEM),
        scratch_shapes=[pltpu.SemaphoreType.DMA((count,))],
    )(jnp.stack(blocks).astype(jnp.int32), activations)


def make_local(n, t):
    bits = n.bit_length() - 1
    links = list(range(1, bits))
    orders = [links, [links[1], links[0], *links[2:]]]
    others = []
    for place in range(n // 2):
        others.append(
            sum(1 << bit for depth, bit in enumerate(links) if (place >> (len(links) - 1 - depth)) & 1)
        )

    def swap(value, bit):
        return lax.ppermute(value, "dp", [(i, i ^ (1 << bit)) for i in range(n)])

    def total(value):
        for bit in reversed(range(bits)):
            value = value + swap(value, bit)
        for bit in range(t.bit_length() - 1):
            value = value + lax.ppermute(value, "tensor", [(i, i ^ (1 << bit)) for i in range(t)])
        return value

    def dot_t(a, g):
        return lax.dot_general(a, g, (((0,), (0,)), ((), ())), preferred_element_type=F32)

    def dot(a, w):
        return lax.dot_general(a, w, (((1,), (0,)), ((), ())), preferred_element_type=F32)

    def local(activations, grad_out, weights, first_moment, second_moment, step):
        rows, kinds, cols = weights.shape
        cut = cols // 2
        parts = [slice(0, cut), slice(cut, cols)]
        count = step[0].astype(F32)
        bias_one = 1.0 - jnp.exp(count * math.log(0.9))
        bias_two = 1.0 - jnp.exp(count * math.log(0.95))
        me = lax.axis_index("dp")

        theirs = pick_blocks(activations, [me ^ (j + 1) for j in others], rows)
        sibling = swap(theirs, 0)
        grads_out = [grad_out[:, s, :] for s in range(kinds)]
        siblings_out = [swap(g, 0) for g in grads_out]
        mine = pick_blocks(after(activations, theirs), [me ^ j for j in others], rows)

        held, got = {}, {}

        def send(s, k, depth, *gates):
            axes = [b for b in links if b not in orders[k][:depth]]
            bit = orders[k][depth]
            axis = axes.index(bit)
            out = lax.index_in_dim(held[s, k], 1, axis, keepdims=False).astype(jnp.float16)
            held[s, k] = lax.index_in_dim(held[s, k], 0, axis, keepdims=False)
            if gates:
                out = after(out, *gates)
            got[s, k, depth] = swap(out, bit)

        def take(s, k, depth, *gates):
            value = got[s, k, depth]
            if gates:
                value = after(value, *gates)
            held[s, k] = held[s, k] + value.astype(F32)

        chunks = range(len(parts))
        deep = len(links)

        def product(s):
            whole = dot_t(mine, grads_out[s]) + dot_t(sibling, siblings_out[s])
            for k in chunks:
                held[s, k] = whole[:, parts[k]].reshape((2,) * deep + (rows, -1))
            return whole

        lead = product(0)
        weights, first_moment, second_moment = (
            after(x, lead) for x in (weights, first_moment, second_moment)
        )
        for k in chunks:
            send(0, k, 0)
        for s in range(1, kinds):
            product(s)
        for depth in range(deep):
            for s in range(kinds):
                if depth == 0 and s > 0:
                    for k in chunks:
                        send(s, k, 0, *[got[s - 1, j, 0] for j in chunks])
                for k in chunks:
                    gates = [got[s - 1, j, depth + 1] for j in chunks] if s > 0 and depth + 1 < deep else []
                    take(s, k, depth, *gates)
                for k in chunks:
                    if depth + 1 < deep:
                        send(s, k, depth + 1)

        weight_sq = jnp.sum(weights * weights, axis=(0, 2))
        ratios, news, kvs = [], [], []
        for s in range(kinds):
            grad = jnp.concatenate([held[s, k] for k in chunks], axis=1)
            first = 0.9 * first_moment[:, s] + 0.1 * grad
            second = 0.95 * second_moment[:, s] + 0.05 * grad * grad
            update = first / bias_one / (jnp.sqrt(second / bias_two) + 1e-06) + 0.1 * weights[:, s]
            update_sq = jnp.sum(update * update)
            if s == 0:
                sums = total(jnp.stack([update_sq, *[weight_sq[i] for i in range(kinds)]]))
                update_total, weight_totals = sums[0], sums[1:]
            else:
                update_total = total(update_sq[None])[0]
            ratio = jnp.sqrt(weight_totals[s]) / (jnp.sqrt(update_total) + 1e-06)
            ratios.append(ratio)
            fresh = weights[:, s] - 0.05 * ratio * update
            news.append((fresh, first, second))
            half_weights = fresh.astype(jnp.bfloat16)
            gathered = [half_weights[:, part] for part in parts]
            for depth in reversed(range(deep)):
                arrived = [swap(gathered[k], orders[k][depth]) for k in chunks]
                for k in chunks:
                    axes = [b for b in links if b not in orders[k][:depth]]
                    axis = axes.index(orders[k][depth])
                    gathered[k] = jnp.stack([gathered[k], arrived[k]], axis=axis)
            for k in chunks:
                own = gathered[k].reshape(-1, gathered[k].shape[-1])
                other = swap(own, 0)
                kvs.append((dot(mine, own) + dot(theirs, other)).astype(jnp.bfloat16))
        new_kv = jnp.concatenate(kvs, axis=1).reshape(-1, kinds, cols)
        new_weights, new_first, new_second = (jnp.stack(x, axis=1) for x in zip(*news))
        return (new_weights, new_first, new_second, jnp.stack(ratios), new_kv)

    return local


def solution(mesh):
    in_specs = (
        P("dp", None),
        P("dp", None, "tensor"),
        P("dp", None, "tensor"),
        P("dp", None, "tensor"),
        P("dp", None, "tensor"),
        P(),
    )
    out_specs = (
        P("dp", None, "tensor"),
        P("dp", None, "tensor"),
        P("dp", None, "tensor"),
        P(),
        P("dp", None, "tensor"),
    )
    local = make_local(mesh.shape["dp"], mesh.shape["tensor"])
    return jax.shard_map(local, mesh=mesh, in_specs=in_specs, out_specs=out_specs, check_vma=False)
```

```python
import math

import jax
import jax.numpy as jnp
from jax import lax
from jax.experimental import pallas as pl
from jax.experimental.layout import Layout, with_layout_constraint
from jax.experimental.pallas import tpu as pltpu
from jax.sharding import PartitionSpec as P

F32 = jnp.float32
LANES = 128
CHUNKS = ((0, 0, 0), (0, 1, 1), (1, 0, 0), (1, 1, 1))


def sums_plan(deep):
    plan = [("P", 0, 0), ("S", 0, 0), ("S", 1, 0), ("P", 1, 0), ("S", 2, 0), ("S", 3, 0)]
    return plan + [("T", i, depth) for depth in range(deep) for i in range(len(CHUNKS))]


def gathers_plan(deep):
    last = deep - 1
    plan = [("G", 0, 0), ("G", 1, 0), ("J", 0, last), ("J", 1, last), ("G", 2, 0), ("G", 3, 0), ("O", 0, 0)]
    for depth in reversed(range(1, last)):
        plan += [("J", 0, depth), ("J", 1, depth), ("J", 2, depth + 1), ("J", 3, depth + 1)]
    plan += [("J", 2, 1), ("J", 3, 1)]
    for pair in ((0, 1), (2, 3)):
        plan += [("J", i, 0) for i in pair]
        plan += [(kind, i, 0) for i in pair for kind in "HK"]
    return plan


def after(value, *others):
    return lax.optimization_barrier((value, *others))[0]


def pick_blocks(activations, others, width):
    half = len(others) // 2
    me = lax.axis_index("dp")
    if width % LANES:
        return [
            jnp.concatenate(
                [lax.dynamic_slice_in_dim(activations, (me ^ j) * width, width, 1) for j in side], axis=1
            )
            for side in (others[:half], others[half:])
        ]
    tokens, count = activations.shape[0], len(others)

    def kernel(src, low, high, held, in_sems, out_sems):
        me = lax.axis_index("dp")
        copies = []
        for i, j in enumerate(others):
            place = held.at[:, pl.ds(i * width, width)]
            block = src.at[:, pl.ds(pl.multiple_of((me ^ j) * width, width), width)]
            dst = (low, high)[i // half].at[:, pl.ds(i % half * width, width)]
            copies.append(
                (
                    pltpu.make_async_copy(block, place, in_sems.at[i]),
                    pltpu.make_async_copy(place, dst, out_sems.at[i]),
                )
            )
        for fetch, _ in copies:
            fetch.start()
        for fetch, store in copies:
            fetch.wait()
            store.start()
        for _, store in copies:
            store.wait()

    return pl.pallas_call(
        kernel,
        out_shape=[jax.ShapeDtypeStruct((tokens, half * width), activations.dtype)] * 2,
        in_specs=[pl.BlockSpec(memory_space=pl.ANY)],
        out_specs=[pl.BlockSpec(memory_space=pl.ANY)] * 2,
        scratch_shapes=[
            pltpu.VMEM((tokens, count * width), activations.dtype),
            pltpu.SemaphoreType.DMA((count,)),
            pltpu.SemaphoreType.DMA((count,)),
        ],
        compiler_params=pltpu.CompilerParams(vmem_limit_bytes=16 * 2**20),
        cost_estimate=pl.CostEstimate(flops=0, bytes_accessed=0, transcendentals=0),
    )(activations)


def multiply(pairs, start=None, over_rows=False, dtype=F32):
    axis = 1 if over_rows else 0
    height, wide = pairs[0][0].shape[axis], pairs[0][1].shape[1]
    tile = math.gcd(height, 256)
    operands = [x for pair in pairs for x in pair] + ([] if start is None else [start])
    dims = (((1 - axis,), (0,)), ((), ()))

    def kernel(*refs):
        *ins, out = refs

        @pl.loop(0, height // tile)
        def _(i):
            here = pl.ds(pl.multiple_of(i * tile, tile), tile)
            value = sum(
                lax.dot_general(
                    a[:, here] if over_rows else a[here, :], b[...], dims, preferred_element_type=F32
                )
                for a, b in zip(ins[0 : 2 * len(pairs) : 2], ins[1 : 2 * len(pairs) : 2])
            )
            if start is not None:
                value = ins[-1][here, :] + value
            out[here, :] = value.astype(dtype)

    return pl.pallas_call(
        kernel,
        out_shape=jax.ShapeDtypeStruct((height, wide), dtype),
        in_specs=[pl.BlockSpec(memory_space=pltpu.VMEM)] * len(operands),
        out_specs=pl.BlockSpec(memory_space=pltpu.VMEM),
        compiler_params=pltpu.CompilerParams(vmem_limit_bytes=24 * 2**20),
        cost_estimate=pl.CostEstimate(flops=0, bytes_accessed=0, transcendentals=0),
    )(*operands)


def rows_first(value):
    return with_layout_constraint(value, Layout(major_to_minor=(0, 1, 2)))


def make_local(n, t):
    bits = n.bit_length() - 1
    links = list(range(1, bits))
    deep = len(links)
    orders = [links, [links[1], links[0], *links[2:]]]

    def blocks_of(order):
        return [
            sum(1 << bit for depth, bit in enumerate(order) if (place >> (deep - 1 - depth)) & 1)
            for place in range(n // 2)
        ]

    def swap(value, bit):
        return lax.ppermute(value, "dp", [(i, i ^ (1 << bit)) for i in range(n)])

    def total(value, fillers):
        hops = [("tensor", bit, t) for bit in range(t.bit_length() - 1)] + [("dp", bit, n) for bit in range(bits)]
        for i, (axis, bit, size) in enumerate(hops):
            other = lax.ppermute(value, axis, [(i, i ^ (1 << bit)) for i in range(size)])
            if i + len(fillers) >= len(hops):
                other = after(other, fillers[i - len(hops)])
            value = value + other
        return value

    def dot_t(a, g):
        return lax.dot_general(a, g, (((0,), (0,)), ((), ())), preferred_element_type=F32)

    def dot(a, w):
        return lax.dot_general(a, w, (((1,), (0,)), ((), ())), preferred_element_type=F32)

    def local(activations, grad_out, weights, first_moment, second_moment, step):
        rows, kinds, cols = weights.shape
        cut = cols // 2
        parts = [slice(0, cut), slice(cut, cols)]
        chunks = [(s, k) for s, k, _ in CHUNKS]
        plans = [plan for *_, plan in CHUNKS]
        amount = len(chunks)
        count = step[0].astype(F32)
        bias_one = 1.0 - jnp.exp(count * math.log(0.9))
        bias_two = 1.0 - jnp.exp(count * math.log(0.95))

        grad_out = lax.optimization_barrier(jnp.transpose(grad_out, (1, 0, 2)))
        shares = blocks_of(orders[0])
        sibling_out = [swap(grad_out[0], 0)]
        theirs = [pick_blocks(after(activations, grad_out), [j + 1 for j in shares], rows)]
        sibling = [swap(side, 0) for side in reversed(theirs[0])][::-1]
        mine = [pick_blocks(after(activations, *theirs[0]), shares, rows)]

        whole, held, got = {}, {}, {}
        last = [grad_out]

        def gated(value):
            return after(value, last[0])

        def product(s):
            if s:
                sibling_out.append(swap(gated(grad_out[s]), 0))
            for side in (1, 0):
                g = gated(grad_out[s])
                pairs = [(mine[0][side], g), (sibling[side], sibling_out[s])]
                if s:
                    whole[s, side] = multiply(pairs, over_rows=True)
                else:
                    whole[s, side] = sum(dot_t(*pair) for pair in pairs)
                last[0] = whole[s, side]

        def halve(i, depth):
            order = orders[plans[i]]
            if depth == 0:
                s, k = chunks[i]
                low, high = (whole[s, side][:, parts[k]] for side in (0, 1))
                if plans[i] == 0:
                    keep, out = low, high
                else:
                    keep, out = (
                        jnp.concatenate(
                            [x.reshape(2, -1, x.shape[1])[side] for x in (low, high)], axis=0
                        )
                        for side in (0, 1)
                    )
            else:
                keep, out = held[i].reshape(2, -1, held[i].shape[1])
            out = out.astype(jnp.float16)
            held[i] = keep
            got[i, depth] = swap(out, order[depth])
            last[0] = out

        def take(i, depth):
            held[i] = held[i] + gated(got[i, depth]).astype(F32)
            if depth + 1 < deep:
                halve(i, depth + 1)
            else:
                last[0] = held[i]

        for kind, i, depth in sums_plan(deep):
            if kind == "P":
                product(i)
            elif kind == "S":
                halve(i, 0)
            else:
                take(i, depth)
                if depth == 0 and i == 0:
                    weights, first_moment, second_moment = (
                        gated(x) for x in (weights, first_moment, second_moment)
                    )
                    theirs.append(pick_blocks(gated(activations), [j + 1 for j in blocks_of(orders[1])], rows))
                    last[0] = theirs[1][0]
                    mine.append(pick_blocks(gated(activations), blocks_of(orders[1]), rows))
                    last[0] = mine[1][0]

        states, sums = [], []
        for s in range(kinds):
            places = sorted((i for i in range(amount) if chunks[i][0] == s), key=lambda i: chunks[i])
            grad = jnp.concatenate([held[i] for i in places], axis=1)
            first = 0.9 * first_moment[:, s] + 0.1 * grad
            second = 0.95 * second_moment[:, s] + 0.05 * grad * grad
            update = first / bias_one / (jnp.sqrt(second / bias_two) + 1e-06) + 0.1 * weights[:, s]
            states.append((first, second, update))
            sums.append(jnp.sum(update * update, axis=0))
        firsts, seconds, updates = zip(*states)
        new_first, new_second = (rows_first(jnp.stack(x, axis=1)) for x in (firsts, seconds))
        weight_sq = jnp.sum(weights * weights, axis=0)
        sums = total(jnp.concatenate([jnp.stack(sums), weight_sq], axis=0), [new_first, new_second])
        sums = jnp.sum(sums, axis=1, keepdims=True)
        ratios = jnp.sqrt(sums[kinds:]) / (jnp.sqrt(sums[:kinds]) + 1e-06)
        scales = lax.optimization_barrier(jnp.broadcast_to(0.05 * ratios, (kinds, cols)))
        ratios = ratios[:, 0]
        news = [weights[:, s] - scales[s][None, :] * updates[s] for s in range(kinds)]
        halves = [fresh.astype(jnp.bfloat16) for fresh in news]
        new_weights = rows_first(jnp.stack(news, axis=1))

        gathered, arrived, sums_of, other, added = {}, {}, {}, {}, set()

        def spread(i, depth):
            arrived[i, depth] = swap(gathered[i], orders[plans[i]][depth])
            last[0] = gathered[i]

        for kind, i, depth in gathers_plan(deep):
            if kind == "G":
                s, k = chunks[i]
                gathered[i] = halves[s][:, parts[k]]
                spread(i, deep - 1)
            elif kind == "O":
                new_weights = gated(new_weights)
                last[0] = new_weights
            elif kind == "J":
                value = gated(arrived[i, depth])
                if depth:
                    gathered[i] = jnp.concatenate([gathered[i], value], axis=0)
                    spread(i, depth - 1)
                else:
                    arrived[i, 0] = value
                    other[i] = swap(jnp.concatenate([gathered[i], value], axis=0), 0)
                    last[0] = value
            elif kind == "H":
                sums_of[i] = multiply([(mine[plans[i]][0], gated(gathered[i]))])
                last[0] = sums_of[i]
            elif kind == "M":
                sums_of[i] = multiply([(mine[plans[i]][1], gated(arrived[i, 0]))], sums_of[i])
                last[0] = sums_of[i]
                added.add(i)
            else:
                pairs = [] if i in added else [(mine[plans[i]][1], arrived[i, 0])]
                sides = gated(other[i]).reshape(2, -1, other[i].shape[1])
                pairs += [(theirs[plans[i]][side], sides[side]) for side in (0, 1)]
                sums_of[i] = multiply(pairs, sums_of[i], dtype=jnp.bfloat16)
                last[0] = sums_of[i]
        places = sorted(range(amount), key=lambda i: chunks[i])
        new_kv = jnp.concatenate([sums_of[i] for i in places], axis=1)
        return (new_weights, new_first, new_second, ratios, new_kv.reshape(-1, kinds, cols))

    return local


def solution(mesh):
    in_specs = (
        P("dp", None),
        P("dp", None, "tensor"),
        P("dp", None, "tensor"),
        P("dp", None, "tensor"),
        P("dp", None, "tensor"),
        P(),
    )
    out_specs = (
        P("dp", None, "tensor"),
        P("dp", None, "tensor"),
        P("dp", None, "tensor"),
        P(),
        P("dp", None, "tensor"),
    )
    local = make_local(mesh.shape["dp"], mesh.shape["tensor"])
    return jax.shard_map(local, mesh=mesh, in_specs=in_specs, out_specs=out_specs, check_vma=False)
```

```python
import math

import jax
import jax.numpy as jnp
from jax import lax
from jax.experimental import pallas as pl
from jax.experimental.layout import Layout, with_layout_constraint
from jax.experimental.pallas import tpu as pltpu
from jax.sharding import PartitionSpec as P

F32 = jnp.float32
LANES = 128
PICK_MIB = 6
DOT_MIB = 8
SUM_CHUNKS = ((0, 0, 2, 0), (0, 2, 4, 1), (1, 0, 2, 0), (1, 2, 4, 1))
GATHER_CHUNKS = ((0, 0, 2, 0), (0, 2, 4, 1), (1, 0, 2, 0), (1, 2, 4, 1))


def sums_plan(deep):
    plan = [("P", 0, 0), ("S", 0, 0), ("S", 1, 0), ("P", 1, 0), ("S", 2, 0), ("S", 3, 0)]
    plan += [("T", i, depth) for depth in range(deep - 1) for i in range(len(SUM_CHUNKS))]
    return plan + [("T", i, deep - 1) for i in (1, 0, 2, 3)]


def gathers_plan(deep):
    last = deep - 1
    plan = [("G", 0, 0), ("G", 1, 0), ("J", 0, last), ("J", 1, last), ("G", 2, 0), ("G", 3, 0)]
    for depth in reversed(range(1, last)):
        plan += [("J", 0, depth), ("J", 1, depth), ("J", 2, depth + 1), ("J", 3, depth + 1)]
    plan += [("O", 0, 0), ("J", 2, 1), ("J", 3, 1), ("J", 0, 0), ("J", 1, 0)]
    plan += [("H", 0, 0), ("K", 0, 0), ("H", 1, 0), ("M", 1, 0), ("K", 1, 0), ("H", 2, 0), ("H", 3, 0)]
    return plan + [("J", 2, 0), ("J", 3, 0), ("M", 2, 0), ("M", 3, 0), ("K", 2, 0), ("K", 3, 0)]


def after(value, *others):
    return lax.optimization_barrier((value, *others))[0]


def pick_blocks(activations, others, width):
    half = len(others) // 2
    me = lax.axis_index("dp")
    if width % LANES:
        return [
            jnp.concatenate(
                [lax.dynamic_slice_in_dim(activations, (me ^ j) * width, width, 1) for j in side], axis=1
            )
            for side in (others[:half], others[half:])
        ]
    tokens, count = activations.shape[0], len(others)

    def kernel(src, low, high, held, in_sems, out_sems):
        me = lax.axis_index("dp")
        copies = []
        for i, j in enumerate(others):
            place = held.at[:, pl.ds(i * width, width)]
            block = src.at[:, pl.ds(pl.multiple_of((me ^ j) * width, width), width)]
            dst = (low, high)[i // half].at[:, pl.ds(i % half * width, width)]
            copies.append(
                (
                    pltpu.make_async_copy(block, place, in_sems.at[i]),
                    pltpu.make_async_copy(place, dst, out_sems.at[i]),
                )
            )
        for fetch, _ in copies:
            fetch.start()
        for fetch, store in copies:
            fetch.wait()
            store.start()
        for _, store in copies:
            store.wait()

    return pl.pallas_call(
        kernel,
        out_shape=[jax.ShapeDtypeStruct((tokens, half * width), activations.dtype)] * 2,
        in_specs=[pl.BlockSpec(memory_space=pl.ANY)],
        out_specs=[pl.BlockSpec(memory_space=pl.ANY)] * 2,
        scratch_shapes=[
            pltpu.VMEM((tokens, count * width), activations.dtype),
            pltpu.SemaphoreType.DMA((count,)),
            pltpu.SemaphoreType.DMA((count,)),
        ],
        compiler_params=pltpu.CompilerParams(vmem_limit_bytes=PICK_MIB * 2**20),
        cost_estimate=pl.CostEstimate(flops=0, bytes_accessed=0, transcendentals=0),
    )(activations)


def multiply(pairs, start=None, over_rows=False, dtype=F32):
    axis = 1 if over_rows else 0
    height, wide = pairs[0][0].shape[axis], pairs[0][1].shape[1]
    tile = math.gcd(height, 256)
    operands = [x for pair in pairs for x in pair] + ([] if start is None else [start])
    dims = (((1 - axis,), (0,)), ((), ()))

    def kernel(*refs):
        *ins, out = refs

        @pl.loop(0, height // tile)
        def _(i):
            here = pl.ds(pl.multiple_of(i * tile, tile), tile)
            value = sum(
                lax.dot_general(
                    a[:, here] if over_rows else a[here, :], b[...], dims, preferred_element_type=F32
                )
                for a, b in zip(ins[0 : 2 * len(pairs) : 2], ins[1 : 2 * len(pairs) : 2])
            )
            if start is not None:
                value = ins[-1][here, :] + value
            out[here, :] = value.astype(dtype)

    return pl.pallas_call(
        kernel,
        out_shape=jax.ShapeDtypeStruct((height, wide), dtype),
        in_specs=[pl.BlockSpec(memory_space=pltpu.VMEM)] * len(operands),
        out_specs=pl.BlockSpec(memory_space=pltpu.VMEM),
        compiler_params=pltpu.CompilerParams(vmem_limit_bytes=DOT_MIB * 2**20),
        cost_estimate=pl.CostEstimate(flops=0, bytes_accessed=0, transcendentals=0),
    )(*operands)


def rows_first(value):
    return with_layout_constraint(value, Layout(major_to_minor=(0, 1, 2)))


def make_local(n, t):
    bits = n.bit_length() - 1
    links = list(range(1, bits))
    deep = len(links)
    orders = [links, [links[1], links[0], *links[2:]]]

    def blocks_of(order):
        return [
            sum(1 << bit for depth, bit in enumerate(order) if (place >> (deep - 1 - depth)) & 1)
            for place in range(n // 2)
        ]

    def swap(value, bit):
        return lax.ppermute(value, "dp", [(i, i ^ (1 << bit)) for i in range(n)])

    def total(value, fillers):
        hops = [("dp", 1 << bit) for bit in range(bits)] + [("tensor", 1 << bit) for bit in range(t.bit_length() - 1)]
        hops = hops[:1] + [hop for pair in zip(hops[bits:], hops[1:bits]) for hop in pair] + [
            hop for hop in hops[1:] if hop not in [x for pair in zip(hops[bits:], hops[1:bits]) for x in pair]
        ]
        rounds = [hops[:1]] + [hops[i : i + 2] for i in range(1, len(hops), 2)]

        def fetch(*flips):
            flip = {"dp": 0, "tensor": 0}
            for axis, amount in flips:
                flip[axis] ^= amount
            perm = [(i, ((i // t) ^ flip["dp"]) * t + ((i % t) ^ flip["tensor"])) for i in range(n * t)]
            return lax.ppermute(value, ("dp", "tensor"), perm)

        for i, around in enumerate(rounds):
            others = [fetch(around[0])]
            if len(around) > 1:
                others += [fetch(around[1]), fetch(*around)]
            if i + len(fillers) >= len(rounds):
                others[0] = after(others[0], fillers[i - len(rounds)])
            value = value + others[0]
            if len(around) > 1:
                value = value + (others[1] + others[2])
        return value

    def dot_t(a, g):
        return lax.dot_general(a, g, (((0,), (0,)), ((), ())), preferred_element_type=F32)

    def dot(a, w):
        return lax.dot_general(a, w, (((1,), (0,)), ((), ())), preferred_element_type=F32)

    def local(activations, grad_out, weights, first_moment, second_moment, step):
        rows, kinds, cols = weights.shape
        chunks = [(s, slice(low * cols // 4, high * cols // 4)) for s, low, high, _ in SUM_CHUNKS]
        plans = [plan for *_, plan in SUM_CHUNKS]
        count = step[0].astype(F32)
        bias_one = 1.0 - jnp.exp(count * math.log(0.9))
        bias_two = 1.0 - jnp.exp(count * math.log(0.95))

        grad_out = lax.optimization_barrier(jnp.transpose(grad_out, (1, 0, 2)))
        sibling_out = [swap(grad_out[0], 0)]
        shares = blocks_of(orders[0])
        theirs = [pick_blocks(after(activations, sibling_out[0]), [j + 1 for j in shares], rows)]
        sibling = [swap(side, 0) for side in reversed(theirs[0])][::-1]
        mine = [pick_blocks(after(activations, *theirs[0]), shares, rows)]

        whole, held, got = {}, {}, {}
        last = [grad_out]

        def gated(value):
            return after(value, last[0])

        def product(s):
            if s:
                sibling_out.append(swap(gated(grad_out[s]), 0))
            for side in (1, 0):
                g = gated(grad_out[s])
                pairs = [(mine[0][side], g), (sibling[side], sibling_out[s])]
                if s:
                    whole[s, side] = multiply(pairs, over_rows=True)
                else:
                    whole[s, side] = sum(dot_t(*pair) for pair in pairs)
                last[0] = whole[s, side]

        def halve(i, depth):
            order = orders[plans[i]]
            if depth == 0:
                s, part = chunks[i]
                low, high = (whole[s, side][:, part] for side in (0, 1))
                if plans[i] == 0:
                    keep, out = low, high
                else:
                    keep, out = (
                        jnp.concatenate(
                            [x.reshape(2, -1, x.shape[1])[side] for x in (low, high)], axis=0
                        )
                        for side in (0, 1)
                    )
            else:
                keep, out = held[i].reshape(2, -1, held[i].shape[1])
            out = out.astype(jnp.float16)
            held[i] = keep
            got[i, depth] = swap(out, order[depth])
            last[0] = out

        def take(i, depth):
            held[i] = held[i] + gated(got[i, depth]).astype(F32)
            if depth + 1 < deep:
                halve(i, depth + 1)
            else:
                last[0] = held[i]

        for kind, i, depth in sums_plan(deep):
            if kind == "P":
                product(i)
            elif kind == "S":
                halve(i, 0)
            else:
                take(i, depth)
                if depth == 0 and i == 0:
                    weights, first_moment, second_moment = (
                        gated(x) for x in (weights, first_moment, second_moment)
                    )
                    theirs.append(pick_blocks(gated(activations), [j + 1 for j in blocks_of(orders[1])], rows))
                    last[0] = theirs[1][0]
                    mine.append(pick_blocks(gated(activations), blocks_of(orders[1]), rows))
                    last[0] = mine[1][0]

        states, sums = [], []
        for s in range(kinds):
            places = sorted((part.start, i) for i, (kind, part) in enumerate(chunks) if kind == s)
            grad = jnp.concatenate([held[i] for _, i in places], axis=1)
            first = 0.9 * first_moment[:, s] + 0.1 * grad
            second = 0.95 * second_moment[:, s] + 0.05 * grad * grad
            update = first / bias_one / (jnp.sqrt(second / bias_two) + 1e-06) + 0.1 * weights[:, s]
            states.append((first, second, update))
            sums.append(jnp.sum(update * update, axis=0))
        firsts, seconds, updates = zip(*states)
        new_first, new_second = (rows_first(jnp.stack(x, axis=1)) for x in (firsts, seconds))
        weight_sq = jnp.sum(weights * weights, axis=0)
        sums = total(jnp.concatenate([jnp.stack(sums), weight_sq], axis=0), [new_first, new_second])
        sums = jnp.sum(sums, axis=1, keepdims=True)
        ratios = jnp.sqrt(sums[kinds:]) / (jnp.sqrt(sums[:kinds]) + 1e-06)
        scales = lax.optimization_barrier(jnp.broadcast_to(0.05 * ratios, (kinds, cols)))
        ratios = ratios[:, 0]
        news = [weights[:, s] - scales[s][None, :] * updates[s] for s in range(kinds)]
        halves = [fresh.astype(jnp.bfloat16) for fresh in news]
        new_weights = rows_first(jnp.stack(news, axis=1))

        chunks = [(s, slice(low * cols // 4, high * cols // 4)) for s, low, high, _ in GATHER_CHUNKS]
        plans = [plan for *_, plan in GATHER_CHUNKS]
        gathered, arrived, sums_of, other, added = {}, {}, {}, {}, set()

        def spread(i, depth):
            arrived[i, depth] = swap(gathered[i], orders[plans[i]][depth])
            last[0] = gathered[i]

        for kind, i, depth in gathers_plan(deep):
            if kind == "G":
                s, part = chunks[i]
                gathered[i] = halves[s][:, part]
                spread(i, deep - 1)
            elif kind == "O":
                new_weights = gated(new_weights)
                last[0] = new_weights
            elif kind == "J":
                value = gated(arrived[i, depth])
                if depth:
                    gathered[i] = jnp.concatenate([gathered[i], value], axis=0)
                    spread(i, depth - 1)
                else:
                    arrived[i, 0] = value
                    other[i] = swap(jnp.concatenate([gathered[i], value], axis=0), 0)
                    last[0] = value
            elif kind == "H":
                sums_of[i] = multiply([(mine[plans[i]][0], gated(gathered[i]))])
                last[0] = sums_of[i]
            elif kind == "M":
                sums_of[i] = multiply([(mine[plans[i]][1], gated(arrived[i, 0]))], sums_of[i])
                last[0] = sums_of[i]
                added.add(i)
            else:
                pairs = [] if i in added else [(mine[plans[i]][1], arrived[i, 0])]
                sides = gated(other[i]).reshape(2, -1, other[i].shape[1])
                pairs += [(theirs[plans[i]][side], sides[side]) for side in (0, 1)]
                sums_of[i] = multiply(pairs, sums_of[i], dtype=jnp.bfloat16)
                last[0] = sums_of[i]
        places = sorted((s, part.start, i) for i, (s, part) in enumerate(chunks))
        new_kv = jnp.concatenate([sums_of[i] for *_, i in places], axis=1)
        return (new_weights, new_first, new_second, ratios, new_kv.reshape(-1, kinds, cols))

    return local


def solution(mesh):
    in_specs = (
        P("dp", None),
        P("dp", None, "tensor"),
        P("dp", None, "tensor"),
        P("dp", None, "tensor"),
        P("dp", None, "tensor"),
        P(),
    )
    out_specs = (
        P("dp", None, "tensor"),
        P("dp", None, "tensor"),
        P("dp", None, "tensor"),
        P(),
        P("dp", None, "tensor"),
    )
    local = make_local(mesh.shape["dp"], mesh.shape["tensor"])
    return jax.shard_map(local, mesh=mesh, in_specs=in_specs, out_specs=out_specs, check_vma=False)
```

```python
import math

import jax
import jax.numpy as jnp
from jax import lax
from jax.experimental import pallas as pl
from jax.experimental.layout import Layout, with_layout_constraint
from jax.experimental.pallas import tpu as pltpu
from jax.sharding import PartitionSpec as P

F32 = jnp.float32
LANES = 128
PLAIN = (2, 3)
PICK_MIB = 6
DOT_MIB = 8
SUM_CHUNKS = ((0, 0, 2, 0), (0, 2, 4, 1), (1, 0, 2, 0), (1, 2, 4, 1))
GATHER_CHUNKS = ((0, 0, 2, 0), (0, 2, 4, 1), (1, 0, 2, 0), (1, 2, 4, 1))


def sums_plan(deep):
    plan = [("P", 0, 1), ("P", 0, 0), ("S", 0, 0), ("S", 1, 0), ("P", 1, 1), ("S", 2, 0), ("P", 1, 0), ("W", 0, 0)]
    plan += [("T", 0, 0), ("S", 3, 0), ("T", 1, 0)]
    for depth in range(1, deep):
        first = [("T", 0, depth), ("T", 1, depth)]
        second = [("T", 2, depth - 1), ("T", 3, depth - 1)]
        plan += [x for pair in zip(first, second) for x in pair] if depth == 1 else second + first
    return plan + [("T", 2, deep - 1), ("T", 3, deep - 1)]


def gathers_plan(deep):
    last = deep - 1
    plan = [("G", 0, 0), ("O", 1, 0), ("G", 1, 0), ("J", 0, last), ("G", 2, 0), ("J", 1, last), ("G", 3, 0)]
    for depth in reversed(range(1, last)):
        plan += [("J", 0, depth), ("J", 1, depth), ("J", 2, depth + 1), ("J", 3, depth + 1)]
    plan += [("O", 0, 0), ("J", 2, 1), ("J", 3, 1), ("J", 0, 0), ("J", 1, 0)]
    plan += [("H", 0, 0), ("K", 0, 0), ("H", 1, 0), ("M", 1, 0), ("K", 1, 0), ("H", 2, 0), ("H", 3, 0), ("O", 2, 0)]
    return plan + [("J", 2, 0), ("J", 3, 0), ("M", 2, 0), ("M", 3, 0), ("K", 2, 0), ("K", 3, 0)]


def after(value, *others):
    return lax.optimization_barrier((value, *others))[0]


def pick_blocks(activations, others, width):
    half = len(others) // 2
    me = lax.axis_index("dp")
    if width % LANES:
        return [
            jnp.concatenate(
                [lax.dynamic_slice_in_dim(activations, (me ^ j) * width, width, 1) for j in side], axis=1
            )
            for side in (others[:half], others[half:])
        ]
    tokens, count = activations.shape[0], len(others)

    def kernel(src, low, high, held, in_sems, out_sems):
        me = lax.axis_index("dp")
        copies = []
        for i, j in enumerate(others):
            place = held.at[:, pl.ds(i * width, width)]
            block = src.at[:, pl.ds(pl.multiple_of((me ^ j) * width, width), width)]
            dst = (low, high)[i // half].at[:, pl.ds(i % half * width, width)]
            copies.append(
                (
                    pltpu.make_async_copy(block, place, in_sems.at[i]),
                    pltpu.make_async_copy(place, dst, out_sems.at[i]),
                )
            )
        for fetch, _ in copies:
            fetch.start()
        for fetch, store in copies:
            fetch.wait()
            store.start()
        for _, store in copies:
            store.wait()

    return pl.pallas_call(
        kernel,
        out_shape=[jax.ShapeDtypeStruct((tokens, half * width), activations.dtype)] * 2,
        in_specs=[pl.BlockSpec(memory_space=pl.ANY)],
        out_specs=[pl.BlockSpec(memory_space=pl.ANY)] * 2,
        scratch_shapes=[
            pltpu.VMEM((tokens, count * width), activations.dtype),
            pltpu.SemaphoreType.DMA((count,)),
            pltpu.SemaphoreType.DMA((count,)),
        ],
        compiler_params=pltpu.CompilerParams(vmem_limit_bytes=PICK_MIB * 2**20),
        cost_estimate=pl.CostEstimate(flops=0, bytes_accessed=0, transcendentals=0),
    )(activations)


def multiply(pairs, start=None, over_rows=False, dtype=F32):
    axis = 1 if over_rows else 0
    height, wide = pairs[0][0].shape[axis], pairs[0][1].shape[1]
    tile = math.gcd(height, 256)
    operands = [x for pair in pairs for x in pair] + ([] if start is None else [start])
    dims = (((1 - axis,), (0,)), ((), ()))

    def kernel(*refs):
        *ins, out = refs

        @pl.loop(0, height // tile)
        def _(i):
            here = pl.ds(pl.multiple_of(i * tile, tile), tile)
            value = sum(
                lax.dot_general(
                    a[:, here] if over_rows else a[here, :], b[...], dims, preferred_element_type=F32
                )
                for a, b in zip(ins[0 : 2 * len(pairs) : 2], ins[1 : 2 * len(pairs) : 2])
            )
            if start is not None:
                value = ins[-1][here, :] + value
            out[here, :] = value.astype(dtype)

    return pl.pallas_call(
        kernel,
        out_shape=jax.ShapeDtypeStruct((height, wide), dtype),
        in_specs=[pl.BlockSpec(memory_space=pltpu.VMEM)] * len(operands),
        out_specs=pl.BlockSpec(memory_space=pltpu.VMEM),
        compiler_params=pltpu.CompilerParams(vmem_limit_bytes=DOT_MIB * 2**20),
        cost_estimate=pl.CostEstimate(flops=0, bytes_accessed=0, transcendentals=0),
    )(*operands)


def rows_first(value):
    return with_layout_constraint(value, Layout(major_to_minor=(0, 1, 2)))


def make_local(n, t):
    bits = n.bit_length() - 1
    links = list(range(1, bits))
    deep = len(links)
    orders = [links, [links[1], links[0], *links[2:]]]

    def blocks_of(order):
        return [
            sum(1 << bit for depth, bit in enumerate(order) if (place >> (deep - 1 - depth)) & 1)
            for place in range(n // 2)
        ]

    def swap(value, bit):
        return lax.ppermute(value, "dp", [(i, i ^ (1 << bit)) for i in range(n)])

    def total(value):
        hops = [("dp", 1 << bit) for bit in range(bits)] + [("tensor", 1 << bit) for bit in range(t.bit_length() - 1)]
        hops = hops[:1] + [hop for pair in zip(hops[bits:], hops[1:bits]) for hop in pair] + [
            hop for hop in hops[1:] if hop not in [x for pair in zip(hops[bits:], hops[1:bits]) for x in pair]
        ]
        rounds = [hops[:1]] + [hops[i : i + 2] for i in range(1, len(hops), 2)]

        def fetch(*flips):
            flip = {"dp": 0, "tensor": 0}
            for axis, amount in flips:
                flip[axis] ^= amount
            perm = [(i, ((i // t) ^ flip["dp"]) * t + ((i % t) ^ flip["tensor"])) for i in range(n * t)]
            return lax.ppermute(value, ("dp", "tensor"), perm)

        for around in rounds:
            others = [fetch(around[0])]
            if len(around) > 1:
                others += [fetch(around[1]), fetch(*around)]
            value = value + others[0]
            if len(around) > 1:
                value = value + (others[1] + others[2])
        return value

    def dot_t(a, g):
        return lax.dot_general(a, g, (((0,), (0,)), ((), ())), preferred_element_type=F32)

    def dot(a, w):
        return lax.dot_general(a, w, (((1,), (0,)), ((), ())), preferred_element_type=F32)

    def local(activations, grad_out, weights, first_moment, second_moment, step):
        rows, kinds, cols = weights.shape
        chunks = [(s, slice(low * cols // 4, high * cols // 4)) for s, low, high, _ in SUM_CHUNKS]
        plans = [plan for *_, plan in SUM_CHUNKS]
        count = step[0].astype(F32)
        bias_one = 1.0 - jnp.exp(count * math.log(0.9))
        bias_two = 1.0 - jnp.exp(count * math.log(0.95))

        grad_out = lax.optimization_barrier(jnp.transpose(grad_out, (1, 0, 2)))
        sibling_out = [swap(grad_out[0], 0)]
        shares = blocks_of(orders[0])
        theirs = [pick_blocks(after(activations, sibling_out[0]), [j + 1 for j in shares], rows)]
        sibling = [swap(side, 0) for side in reversed(theirs[0])][::-1]
        mine = [pick_blocks(after(activations, *theirs[0]), shares, rows)]

        whole, held, got = {}, {}, {}
        last = [grad_out]

        def gated(value):
            return after(value, last[0])

        def product(s, side):
            if len(sibling_out) <= s:
                sibling_out.append(swap(gated(grad_out[s]), 0))
            g = gated(grad_out[s])
            pairs = [(mine[0][side], g), (sibling[side], sibling_out[s])]
            if s:
                whole[s, side] = multiply(pairs, over_rows=True)
            else:
                whole[s, side] = sum(dot_t(*pair) for pair in pairs)
            last[0] = whole[s, side]

        def halve(i, depth):
            order = orders[plans[i]]
            if depth == 0:
                s, part = chunks[i]
                if plans[i] == 0:
                    out = whole[s, 1][:, part]
                else:
                    low, high = (whole[s, side][:, part] for side in (0, 1))
                    held[i], out = (
                        jnp.concatenate(
                            [x.reshape(2, -1, x.shape[1])[side] for x in (low, high)], axis=0
                        )
                        for side in (0, 1)
                    )
            else:
                held[i], out = held[i].reshape(2, -1, held[i].shape[1])
            out = out.astype(jnp.float16)
            if depth == 0:
                out = gated(out)
            got[i, depth] = swap(out, order[depth])
            last[0] = out

        def take(i, depth):
            if depth == 0 and plans[i] == 0:
                s, part = chunks[i]
                held[i] = whole[s, 0][:, part]
            held[i] = held[i] + gated(got[i, depth]).astype(F32)
            if depth + 1 < deep:
                halve(i, depth + 1)
            else:
                last[0] = held[i]

        for kind, i, depth in sums_plan(deep):
            if kind == "P":
                product(i, depth)
            elif kind == "S":
                halve(i, 0)
            elif kind == "T":
                take(i, depth)
            else:
                weights, first_moment, second_moment = (
                    gated(x) for x in (weights, first_moment, second_moment)
                )
                theirs.append(pick_blocks(gated(activations), [j + 1 for j in blocks_of(orders[1])], rows))
                last[0] = theirs[1][0]
                mine.append(pick_blocks(gated(activations), blocks_of(orders[1]), rows))
                last[0] = mine[1][0]

        states, sums = [], []
        for s in range(kinds):
            places = sorted((part.start, i) for i, (kind, part) in enumerate(chunks) if kind == s)
            grad = jnp.concatenate([held[i] for _, i in places], axis=1)
            first = 0.9 * first_moment[:, s] + 0.1 * grad
            second = 0.95 * second_moment[:, s] + 0.05 * grad * grad
            update = first / bias_one / (jnp.sqrt(second / bias_two) + 1e-06) + 0.1 * weights[:, s]
            states.append((first, second, update))
            sums.append(jnp.sum(update * update, axis=0))
        firsts, seconds, updates = zip(*states)
        new_first, new_second = (jnp.stack(x, axis=1) for x in (firsts, seconds))
        weight_sq = jnp.sum(weights * weights, axis=0)
        sums = total(jnp.concatenate([jnp.stack(sums), weight_sq], axis=0))
        sums = jnp.sum(sums, axis=1, keepdims=True)
        ratios = jnp.sqrt(sums[kinds:]) / (jnp.sqrt(sums[:kinds]) + 1e-06)
        scales = lax.optimization_barrier(jnp.broadcast_to(0.05 * ratios, (kinds, cols)))
        ratios = ratios[:, 0]
        news = [weights[:, s] - scales[s][None, :] * updates[s] for s in range(kinds)]
        halves = [fresh.astype(jnp.bfloat16) for fresh in news]
        outs = [jnp.stack(news, axis=1), new_first, new_second]

        chunks = [(s, slice(low * cols // 4, high * cols // 4)) for s, low, high, _ in GATHER_CHUNKS]
        plans = [plan for *_, plan in GATHER_CHUNKS]
        gathered, arrived, sums_of, other, added = {}, {}, {}, {}, set()

        def spread(i, depth):
            arrived[i, depth] = swap(gathered[i], orders[plans[i]][depth])
            last[0] = gathered[i]

        for kind, i, depth in gathers_plan(deep):
            if kind == "G":
                s, part = chunks[i]
                gathered[i] = gated(halves[s][:, part])
                spread(i, deep - 1)
            elif kind == "O":
                outs[i] = rows_first(gated(outs[i]))
                last[0] = outs[i]
            elif kind == "J":
                value = gated(arrived[i, depth])
                if depth:
                    gathered[i] = jnp.concatenate([gathered[i], value], axis=0)
                    spread(i, depth - 1)
                else:
                    arrived[i, 0] = value
                    other[i] = swap(jnp.concatenate([gathered[i], value], axis=0), 0)
                    last[0] = value
            elif kind == "H":
                sums_of[i] = multiply([(mine[plans[i]][0], gated(gathered[i]))])
                last[0] = sums_of[i]
            elif kind == "M":
                if i in PLAIN:
                    sums_of[i] = sums_of[i] + dot(mine[plans[i]][1], gated(arrived[i, 0]))
                else:
                    sums_of[i] = multiply([(mine[plans[i]][1], gated(arrived[i, 0]))], sums_of[i])
                last[0] = sums_of[i]
                added.add(i)
            else:
                pairs = [] if i in added else [(mine[plans[i]][1], arrived[i, 0])]
                sides = gated(other[i]).reshape(2, -1, other[i].shape[1])
                pairs += [(theirs[plans[i]][side], sides[side]) for side in (0, 1)]
                if i in PLAIN:
                    sums_of[i] = sum((dot(*pair) for pair in pairs), sums_of[i]).astype(jnp.bfloat16)
                else:
                    sums_of[i] = multiply(pairs, sums_of[i], dtype=jnp.bfloat16)
                last[0] = sums_of[i]
        places = sorted((s, part.start, i) for i, (s, part) in enumerate(chunks))
        new_kv = jnp.concatenate([sums_of[i] for *_, i in places], axis=1)
        return (*outs, ratios, new_kv.reshape(-1, kinds, cols))

    return local


def solution(mesh):
    in_specs = (
        P("dp", None),
        P("dp", None, "tensor"),
        P("dp", None, "tensor"),
        P("dp", None, "tensor"),
        P("dp", None, "tensor"),
        P(),
    )
    out_specs = (
        P("dp", None, "tensor"),
        P("dp", None, "tensor"),
        P("dp", None, "tensor"),
        P(),
        P("dp", None, "tensor"),
    )
    local = make_local(mesh.shape["dp"], mesh.shape["tensor"])
    return jax.shard_map(local, mesh=mesh, in_specs=in_specs, out_specs=out_specs, check_vma=False)
```

```python
import math

import jax
import jax.numpy as jnp
from jax import lax
from jax.experimental import pallas as pl
from jax.experimental.layout import Layout, with_layout_constraint
from jax.experimental.pallas import tpu as pltpu
from jax.sharding import PartitionSpec as P

F32 = jnp.float32
LANES = 128
PLAIN = (2, 3)
PICK_MIB = 6
DOT_MIB = 8
SUM_CHUNKS = ((0, 0, 2, 0), (0, 2, 4, 1), (1, 0, 2, 0), (1, 2, 4, 1))
GATHER_CHUNKS = ((0, 0, 2, 0), (0, 2, 4, 1), (1, 0, 2, 0), (1, 2, 4, 1))


def sums_plan(deep):
    plan = [("P", 0, 1), ("P", 0, 0), ("S", 0, 0), ("S", 1, 0), ("P", 1, 1), ("S", 2, 0), ("P", 1, 0), ("W", 0, 0)]
    plan += [("T", 0, 0), ("S", 3, 0), ("T", 1, 0)]
    for depth in range(1, deep):
        first = [("T", 0, depth), ("T", 1, depth)]
        second = [("T", 2, depth - 1), ("T", 3, depth - 1)]
        plan += [x for pair in zip(first, second) for x in pair] if depth == 1 else second + first
    return plan + [("T", 2, deep - 1), ("T", 3, deep - 1)]


def gathers_plan(deep):
    last = deep - 1
    plan = [("G", 0, 0), ("O", 1, 0), ("G", 1, 0), ("J", 0, last), ("G", 2, 0), ("J", 1, last), ("G", 3, 0)]
    for depth in reversed(range(1, last)):
        plan += [("J", 0, depth), ("J", 1, depth), ("J", 2, depth + 1), ("J", 3, depth + 1)]
    plan += [("O", 0, 0), ("J", 2, 1), ("J", 3, 1), ("J", 0, 0), ("J", 1, 0)]
    plan += [("H", 0, 0), ("K", 0, 0), ("H", 1, 0), ("M", 1, 0), ("K", 1, 0), ("H", 2, 0), ("H", 3, 0), ("O", 2, 0)]
    return plan + [("J", 2, 0), ("J", 3, 0), ("M", 2, 0), ("M", 3, 0), ("K", 2, 0), ("K", 3, 0)]


def after(value, *others):
    return lax.optimization_barrier((value, *others))[0]


def pick_blocks(activations, others, width):
    half = len(others) // 2
    me = lax.axis_index("dp")
    if width % LANES:
        return [
            jnp.concatenate(
                [lax.dynamic_slice_in_dim(activations, (me ^ j) * width, width, 1) for j in side], axis=1
            )
            for side in (others[:half], others[half:])
        ]
    tokens, count = activations.shape[0], len(others)

    def kernel(src, low, high, held, in_sems, out_sems):
        me = lax.axis_index("dp")
        copies = []
        for i, j in enumerate(others):
            place = held.at[:, pl.ds(i * width, width)]
            block = src.at[:, pl.ds(pl.multiple_of((me ^ j) * width, width), width)]
            dst = (low, high)[i // half].at[:, pl.ds(i % half * width, width)]
            copies.append(
                (
                    pltpu.make_async_copy(block, place, in_sems.at[i]),
                    pltpu.make_async_copy(place, dst, out_sems.at[i]),
                )
            )
        for fetch, _ in copies:
            fetch.start()
        for fetch, store in copies:
            fetch.wait()
            store.start()
        for _, store in copies:
            store.wait()

    return pl.pallas_call(
        kernel,
        out_shape=[jax.ShapeDtypeStruct((tokens, half * width), activations.dtype)] * 2,
        in_specs=[pl.BlockSpec(memory_space=pl.ANY)],
        out_specs=[pl.BlockSpec(memory_space=pl.ANY)] * 2,
        scratch_shapes=[
            pltpu.VMEM((tokens, count * width), activations.dtype),
            pltpu.SemaphoreType.DMA((count,)),
            pltpu.SemaphoreType.DMA((count,)),
        ],
        compiler_params=pltpu.CompilerParams(vmem_limit_bytes=PICK_MIB * 2**20),
        cost_estimate=pl.CostEstimate(flops=0, bytes_accessed=0, transcendentals=0),
    )(activations)


def multiply(pairs, start=None, over_rows=False, dtype=F32):
    axis = 1 if over_rows else 0
    height, wide = pairs[0][0].shape[axis], pairs[0][1].shape[1]
    tile = math.gcd(height, 256)
    operands = [x for pair in pairs for x in pair] + ([] if start is None else [start])
    dims = (((1 - axis,), (0,)), ((), ()))

    def kernel(*refs):
        *ins, out = refs

        @pl.loop(0, height // tile)
        def _(i):
            here = pl.ds(pl.multiple_of(i * tile, tile), tile)
            value = sum(
                lax.dot_general(
                    a[:, here] if over_rows else a[here, :], b[...], dims, preferred_element_type=F32
                )
                for a, b in zip(ins[0 : 2 * len(pairs) : 2], ins[1 : 2 * len(pairs) : 2])
            )
            if start is not None:
                value = ins[-1][here, :] + value
            out[here, :] = value.astype(dtype)

    return pl.pallas_call(
        kernel,
        out_shape=jax.ShapeDtypeStruct((height, wide), dtype),
        in_specs=[pl.BlockSpec(memory_space=pltpu.VMEM)] * len(operands),
        out_specs=pl.BlockSpec(memory_space=pltpu.VMEM),
        compiler_params=pltpu.CompilerParams(vmem_limit_bytes=DOT_MIB * 2**20),
        cost_estimate=pl.CostEstimate(flops=0, bytes_accessed=0, transcendentals=0),
    )(*operands)


def rows_first(value):
    return with_layout_constraint(value, Layout(major_to_minor=(0, 1, 2)))


def make_local(n, t):
    bits = n.bit_length() - 1
    links = list(range(1, bits))
    deep = len(links)
    orders = [links, [links[1], links[0], *links[2:]]]

    def blocks_of(order):
        return [
            sum(1 << bit for depth, bit in enumerate(order) if (place >> (deep - 1 - depth)) & 1)
            for place in range(n // 2)
        ]

    def swap(value, bit):
        return lax.ppermute(value, "dp", [(i, i ^ (1 << bit)) for i in range(n)])

    def total(value):
        hops = [("dp", 0, n)]
        hops += [("tensor", bit, t) for bit in range(t.bit_length() - 1)]
        hops += [("dp", bit, n) for bit in links]
        for axis, bit, size in hops:
            value = value + lax.ppermute(value, axis, [(i, i ^ (1 << bit)) for i in range(size)])
        return value

    def dot_t(a, g):
        return lax.dot_general(a, g, (((0,), (0,)), ((), ())), preferred_element_type=F32)

    def dot(a, w):
        return lax.dot_general(a, w, (((1,), (0,)), ((), ())), preferred_element_type=F32)

    def local(activations, grad_out, weights, first_moment, second_moment, step):
        rows, kinds, cols = weights.shape
        chunks = [(s, slice(low * cols // 4, high * cols // 4)) for s, low, high, _ in SUM_CHUNKS]
        plans = [plan for *_, plan in SUM_CHUNKS]
        count = step[0].astype(F32)
        bias_one = 1.0 - jnp.exp(count * math.log(0.9))
        bias_two = 1.0 - jnp.exp(count * math.log(0.95))

        grad_out = lax.optimization_barrier(jnp.transpose(grad_out, (1, 0, 2)))
        sibling_out = [swap(grad_out[0], 0)]
        shares = blocks_of(orders[0])
        theirs = [pick_blocks(after(activations, sibling_out[0]), [j + 1 for j in shares], rows)]
        sibling = [swap(side, 0) for side in reversed(theirs[0])][::-1]
        mine = [pick_blocks(after(activations, *theirs[0]), shares, rows)]

        whole, held, got = {}, {}, {}
        last = [grad_out]

        def gated(value):
            return after(value, last[0])

        def product(s, side):
            if len(sibling_out) <= s:
                sibling_out.append(swap(gated(grad_out[s]), 0))
            g = gated(grad_out[s])
            pairs = [(mine[0][side], g), (sibling[side], sibling_out[s])]
            if s:
                whole[s, side] = multiply(pairs, over_rows=True)
            else:
                whole[s, side] = sum(dot_t(*pair) for pair in pairs)
            last[0] = whole[s, side]

        def halve(i, depth):
            order = orders[plans[i]]
            if depth == 0:
                s, part = chunks[i]
                if plans[i] == 0:
                    out = whole[s, 1][:, part]
                else:
                    low, high = (whole[s, side][:, part] for side in (0, 1))
                    held[i], out = (
                        jnp.concatenate(
                            [x.reshape(2, -1, x.shape[1])[side] for x in (low, high)], axis=0
                        )
                        for side in (0, 1)
                    )
            else:
                held[i], out = held[i].reshape(2, -1, held[i].shape[1])
            out = out.astype(jnp.float16)
            if depth == 0:
                out = gated(out)
            got[i, depth] = swap(out, order[depth])
            last[0] = out

        def take(i, depth):
            if depth == 0 and plans[i] == 0:
                s, part = chunks[i]
                held[i] = whole[s, 0][:, part]
            held[i] = held[i] + gated(got[i, depth]).astype(F32)
            if depth + 1 < deep:
                halve(i, depth + 1)
            else:
                last[0] = held[i]

        for kind, i, depth in sums_plan(deep):
            if kind == "P":
                product(i, depth)
            elif kind == "S":
                halve(i, 0)
            elif kind == "T":
                take(i, depth)
            else:
                weights, first_moment, second_moment = (
                    gated(x) for x in (weights, first_moment, second_moment)
                )
                theirs.append(pick_blocks(gated(activations), [j + 1 for j in blocks_of(orders[1])], rows))
                last[0] = theirs[1][0]
                mine.append(pick_blocks(gated(activations), blocks_of(orders[1]), rows))
                last[0] = mine[1][0]

        states, sums = [], []
        for s in range(kinds):
            places = sorted((part.start, i) for i, (kind, part) in enumerate(chunks) if kind == s)
            grad = jnp.concatenate([held[i] for _, i in places], axis=1)
            first = 0.9 * first_moment[:, s] + 0.1 * grad
            second = 0.95 * second_moment[:, s] + 0.05 * grad * grad
            update = first / bias_one / (jnp.sqrt(second / bias_two) + 1e-06) + 0.1 * weights[:, s]
            states.append((first, second, update))
            sums.append(jnp.sum(update * update, axis=0))
        firsts, seconds, updates = zip(*states)
        new_first, new_second = (jnp.stack(x, axis=1) for x in (firsts, seconds))
        weight_sq = jnp.sum(weights * weights, axis=0)
        sums = total(jnp.concatenate([jnp.stack(sums), weight_sq], axis=0))
        sums = jnp.sum(sums, axis=1, keepdims=True)
        ratios = jnp.sqrt(sums[kinds:]) / (jnp.sqrt(sums[:kinds]) + 1e-06)
        scales = lax.optimization_barrier(jnp.broadcast_to(0.05 * ratios, (kinds, cols)))
        ratios = ratios[:, 0]
        news = [weights[:, s] - scales[s][None, :] * updates[s] for s in range(kinds)]
        halves = [fresh.astype(jnp.bfloat16) for fresh in news]
        outs = [jnp.stack(news, axis=1), new_first, new_second]

        chunks = [(s, slice(low * cols // 4, high * cols // 4)) for s, low, high, _ in GATHER_CHUNKS]
        plans = [plan for *_, plan in GATHER_CHUNKS]
        gathered, arrived, sums_of, other, added = {}, {}, {}, {}, set()

        def spread(i, depth):
            arrived[i, depth] = swap(gathered[i], orders[plans[i]][depth])
            last[0] = gathered[i]

        for kind, i, depth in gathers_plan(deep):
            if kind == "G":
                s, part = chunks[i]
                gathered[i] = gated(halves[s][:, part])
                spread(i, deep - 1)
            elif kind == "O":
                outs[i] = rows_first(gated(outs[i]))
                last[0] = outs[i]
            elif kind == "J":
                value = gated(arrived[i, depth])
                if depth:
                    gathered[i] = jnp.concatenate([gathered[i], value], axis=0)
                    spread(i, depth - 1)
                else:
                    arrived[i, 0] = value
                    other[i] = swap(jnp.concatenate([gathered[i], value], axis=0), 0)
                    last[0] = value
            elif kind == "H":
                sums_of[i] = multiply([(mine[plans[i]][0], gated(gathered[i]))])
                last[0] = sums_of[i]
            elif kind == "M":
                if i in PLAIN:
                    sums_of[i] = sums_of[i] + dot(mine[plans[i]][1], gated(arrived[i, 0]))
                else:
                    sums_of[i] = multiply([(mine[plans[i]][1], gated(arrived[i, 0]))], sums_of[i])
                last[0] = sums_of[i]
                added.add(i)
            else:
                pairs = [] if i in added else [(mine[plans[i]][1], arrived[i, 0])]
                sides = gated(other[i]).reshape(2, -1, other[i].shape[1])
                pairs += [(theirs[plans[i]][side], sides[side]) for side in (0, 1)]
                if i in PLAIN:
                    sums_of[i] = sum((dot(*pair) for pair in pairs), sums_of[i]).astype(jnp.bfloat16)
                else:
                    sums_of[i] = multiply(pairs, sums_of[i], dtype=jnp.bfloat16)
                last[0] = sums_of[i]
        places = sorted((s, part.start, i) for i, (s, part) in enumerate(chunks))
        new_kv = jnp.concatenate([sums_of[i] for *_, i in places], axis=1)
        return (*outs, ratios, new_kv.reshape(-1, kinds, cols))

    return local


def solution(mesh):
    in_specs = (
        P("dp", None),
        P("dp", None, "tensor"),
        P("dp", None, "tensor"),
        P("dp", None, "tensor"),
        P("dp", None, "tensor"),
        P(),
    )
    out_specs = (
        P("dp", None, "tensor"),
        P("dp", None, "tensor"),
        P("dp", None, "tensor"),
        P(),
        P("dp", None, "tensor"),
    )
    local = make_local(mesh.shape["dp"], mesh.shape["tensor"])
    return jax.shard_map(local, mesh=mesh, in_specs=in_specs, out_specs=out_specs, check_vma=False)
```

```python
import math

import jax
import jax.numpy as jnp
from jax import lax
from jax.experimental import pallas as pl
from jax.experimental.layout import Layout, with_layout_constraint
from jax.experimental.pallas import tpu as pltpu
from jax.sharding import PartitionSpec as P

F32 = jnp.float32
LANES = 128
PLAIN = (2, 3)
PICK_MIB = 6
DOT_MIB = 8
SUM_CHUNKS = ((0, 0, 2, 0), (0, 2, 4, 1), (1, 0, 2, 0), (1, 2, 4, 1))
GATHER_CHUNKS = ((0, 0, 2, 0), (0, 2, 4, 1), (1, 0, 2, 0), (1, 2, 4, 1))


def sums_plan(deep):
    plan = [("P", 0, 1), ("P", 0, 0), ("S", 0, 0), ("S", 1, 0), ("P", 1, 1), ("S", 2, 0), ("P", 1, 0), ("W", 0, 0)]
    plan += [("T", 0, 0), ("S", 3, 0), ("T", 1, 0)]
    for depth in range(1, deep):
        first = [("T", 0, depth), ("T", 1, depth)]
        second = [("T", 2, depth - 1), ("T", 3, depth - 1)]
        plan += [x for pair in zip(first, second) for x in pair] if depth == 1 else second + first
    return plan + [("T", 2, deep - 1), ("T", 3, deep - 1)]


def gathers_plan(deep):
    last = deep - 1
    plan = [("G", 0, 0), ("O", 1, 0), ("G", 1, 0), ("J", 0, last), ("G", 2, 0), ("J", 1, last), ("G", 3, 0)]
    for depth in reversed(range(1, last)):
        plan += [("J", 0, depth), ("J", 2, depth + 1), ("J", 1, depth), ("J", 3, depth + 1)]
    plan += [("O", 0, 0), ("J", 2, 1), ("J", 3, 1), ("J", 0, 0), ("J", 1, 0)]
    plan += [("H", 0, 0), ("K", 0, 0), ("H", 1, 0), ("M", 1, 0), ("K", 1, 0), ("H", 2, 0), ("H", 3, 0), ("O", 2, 0)]
    return plan + [("J", 2, 0), ("J", 3, 0), ("M", 2, 0), ("M", 3, 0), ("K", 2, 0), ("K", 3, 0)]


def after(value, *others):
    return lax.optimization_barrier((value, *others))[0]


def pick_blocks(activations, others, width):
    half = len(others) // 2
    me = lax.axis_index("dp")
    if width % LANES:
        return [
            jnp.concatenate(
                [lax.dynamic_slice_in_dim(activations, (me ^ j) * width, width, 1) for j in side], axis=1
            )
            for side in (others[:half], others[half:])
        ]
    tokens, count = activations.shape[0], len(others)

    def kernel(src, low, high, held, in_sems, out_sems):
        me = lax.axis_index("dp")
        copies = []
        for i, j in enumerate(others):
            place = held.at[:, pl.ds(i * width, width)]
            block = src.at[:, pl.ds(pl.multiple_of((me ^ j) * width, width), width)]
            dst = (low, high)[i // half].at[:, pl.ds(i % half * width, width)]
            copies.append(
                (
                    pltpu.make_async_copy(block, place, in_sems.at[i]),
                    pltpu.make_async_copy(place, dst, out_sems.at[i]),
                )
            )
        for fetch, _ in copies:
            fetch.start()
        for fetch, store in copies:
            fetch.wait()
            store.start()
        for _, store in copies:
            store.wait()

    return pl.pallas_call(
        kernel,
        out_shape=[jax.ShapeDtypeStruct((tokens, half * width), activations.dtype)] * 2,
        in_specs=[pl.BlockSpec(memory_space=pl.ANY)],
        out_specs=[pl.BlockSpec(memory_space=pl.ANY)] * 2,
        scratch_shapes=[
            pltpu.VMEM((tokens, count * width), activations.dtype),
            pltpu.SemaphoreType.DMA((count,)),
            pltpu.SemaphoreType.DMA((count,)),
        ],
        compiler_params=pltpu.CompilerParams(vmem_limit_bytes=PICK_MIB * 2**20),
        cost_estimate=pl.CostEstimate(flops=0, bytes_accessed=0, transcendentals=0),
    )(activations)


def multiply(pairs, start=None, over_rows=False, dtype=F32):
    axis = 1 if over_rows else 0
    height, wide = pairs[0][0].shape[axis], pairs[0][1].shape[1]
    tile = math.gcd(height, 256)
    operands = [x for pair in pairs for x in pair] + ([] if start is None else [start])
    dims = (((1 - axis,), (0,)), ((), ()))

    def kernel(*refs):
        *ins, out = refs

        @pl.loop(0, height // tile)
        def _(i):
            here = pl.ds(pl.multiple_of(i * tile, tile), tile)
            value = sum(
                lax.dot_general(
                    a[:, here] if over_rows else a[here, :], b[...], dims, preferred_element_type=F32
                )
                for a, b in zip(ins[0 : 2 * len(pairs) : 2], ins[1 : 2 * len(pairs) : 2])
            )
            if start is not None:
                value = ins[-1][here, :] + value
            out[here, :] = value.astype(dtype)

    return pl.pallas_call(
        kernel,
        out_shape=jax.ShapeDtypeStruct((height, wide), dtype),
        in_specs=[pl.BlockSpec(memory_space=pltpu.VMEM)] * len(operands),
        out_specs=pl.BlockSpec(memory_space=pltpu.VMEM),
        compiler_params=pltpu.CompilerParams(vmem_limit_bytes=DOT_MIB * 2**20),
        cost_estimate=pl.CostEstimate(flops=0, bytes_accessed=0, transcendentals=0),
    )(*operands)


def rows_first(value):
    return with_layout_constraint(value, Layout(major_to_minor=(0, 1, 2)))


def make_local(n, t):
    bits = n.bit_length() - 1
    links = list(range(1, bits))
    deep = len(links)
    orders = [links, [links[1], links[0], *links[2:]]]

    def blocks_of(order):
        return [
            sum(1 << bit for depth, bit in enumerate(order) if (place >> (deep - 1 - depth)) & 1)
            for place in range(n // 2)
        ]

    def swap(value, bit):
        return lax.ppermute(value, "dp", [(i, i ^ (1 << bit)) for i in range(n)])

    def total(value):
        hops = [("dp", 0, n)]
        hops += [("tensor", bit, t) for bit in range(t.bit_length() - 1)]
        hops += [("dp", bit, n) for bit in links]
        for axis, bit, size in hops:
            value = value + lax.ppermute(value, axis, [(i, i ^ (1 << bit)) for i in range(size)])
        return value

    def dot_t(a, g):
        return lax.dot_general(a, g, (((0,), (0,)), ((), ())), preferred_element_type=F32)

    def dot(a, w):
        return lax.dot_general(a, w, (((1,), (0,)), ((), ())), preferred_element_type=F32)

    def local(activations, grad_out, weights, first_moment, second_moment, step):
        rows, kinds, cols = weights.shape
        chunks = [(s, slice(low * cols // 4, high * cols // 4)) for s, low, high, _ in SUM_CHUNKS]
        plans = [plan for *_, plan in SUM_CHUNKS]
        count = step[0].astype(F32)
        bias_one = 1.0 - jnp.exp(count * math.log(0.9))
        bias_two = 1.0 - jnp.exp(count * math.log(0.95))

        grad_out = lax.optimization_barrier(jnp.transpose(grad_out, (1, 0, 2)))
        sibling_out = [swap(grad_out[0], 0)]
        shares = blocks_of(orders[0])
        theirs = [pick_blocks(after(activations, sibling_out[0]), [j + 1 for j in shares], rows)]
        sibling = [swap(side, 0) for side in reversed(theirs[0])][::-1]
        mine = [pick_blocks(after(activations, *theirs[0]), shares, rows)]

        whole, held, got = {}, {}, {}
        last = [grad_out]

        def gated(value):
            return after(value, last[0])

        def product(s, side):
            if len(sibling_out) <= s:
                sibling_out.append(swap(gated(grad_out[s]), 0))
            g = gated(grad_out[s])
            pairs = [(mine[0][side], g), (sibling[side], sibling_out[s])]
            if s:
                whole[s, side] = multiply(pairs, over_rows=True)
            else:
                whole[s, side] = sum(dot_t(*pair) for pair in pairs)
            last[0] = whole[s, side]

        def halve(i, depth):
            order = orders[plans[i]]
            if depth == 0:
                s, part = chunks[i]
                if plans[i] == 0:
                    out = whole[s, 1][:, part]
                else:
                    low, high = (whole[s, side][:, part] for side in (0, 1))
                    held[i], out = (
                        jnp.concatenate(
                            [x.reshape(2, -1, x.shape[1])[side] for x in (low, high)], axis=0
                        )
                        for side in (0, 1)
                    )
            else:
                held[i], out = held[i].reshape(2, -1, held[i].shape[1])
            out = out.astype(jnp.float16)
            if depth == 0:
                out = gated(out)
            got[i, depth] = swap(out, order[depth])
            last[0] = out

        def take(i, depth):
            if depth == 0 and plans[i] == 0:
                s, part = chunks[i]
                held[i] = whole[s, 0][:, part]
            held[i] = held[i] + gated(got[i, depth]).astype(F32)
            if depth + 1 < deep:
                halve(i, depth + 1)
            else:
                last[0] = held[i]

        for kind, i, depth in sums_plan(deep):
            if kind == "P":
                product(i, depth)
            elif kind == "S":
                halve(i, 0)
            elif kind == "T":
                take(i, depth)
            else:
                weights, first_moment, second_moment = (
                    gated(x) for x in (weights, first_moment, second_moment)
                )
                theirs.append(pick_blocks(gated(activations), [j + 1 for j in blocks_of(orders[1])], rows))
                last[0] = theirs[1][0]
                mine.append(pick_blocks(gated(activations), blocks_of(orders[1]), rows))
                last[0] = mine[1][0]

        states, sums = [], []
        for s in range(kinds):
            places = sorted((part.start, i) for i, (kind, part) in enumerate(chunks) if kind == s)
            grad = jnp.concatenate([held[i] for _, i in places], axis=1)
            first = 0.9 * first_moment[:, s] + 0.1 * grad
            second = 0.95 * second_moment[:, s] + 0.05 * grad * grad
            update = first / bias_one / (jnp.sqrt(second / bias_two) + 1e-06) + 0.1 * weights[:, s]
            states.append((first, second, update))
            sums.append(jnp.sum(update * update, axis=0))
        firsts, seconds, updates = zip(*states)
        new_first, new_second = (jnp.stack(x, axis=1) for x in (firsts, seconds))
        weight_sq = jnp.sum(weights * weights, axis=0)
        sums = total(jnp.concatenate([jnp.stack(sums), weight_sq], axis=0))
        sums = jnp.sum(sums, axis=1, keepdims=True)
        ratios = jnp.sqrt(sums[kinds:]) / (jnp.sqrt(sums[:kinds]) + 1e-06)
        scales = lax.optimization_barrier(jnp.broadcast_to(0.05 * ratios, (kinds, cols)))
        ratios = ratios[:, 0]
        news = [weights[:, s] - scales[s][None, :] * updates[s] for s in range(kinds)]
        halves = [fresh.astype(jnp.bfloat16) for fresh in news]
        outs = [jnp.stack(news, axis=1), new_first, new_second]

        chunks = [(s, slice(low * cols // 4, high * cols // 4)) for s, low, high, _ in GATHER_CHUNKS]
        plans = [plan for *_, plan in GATHER_CHUNKS]
        gathered, arrived, sums_of, other, added = {}, {}, {}, {}, set()

        def spread(i, depth):
            arrived[i, depth] = swap(gathered[i], orders[plans[i]][depth])
            last[0] = gathered[i]

        for kind, i, depth in gathers_plan(deep):
            if kind == "G":
                s, part = chunks[i]
                gathered[i] = gated(halves[s][:, part])
                spread(i, deep - 1)
            elif kind == "O":
                outs[i] = rows_first(gated(outs[i]))
                last[0] = outs[i]
            elif kind == "J":
                value = gated(arrived[i, depth])
                if depth:
                    gathered[i] = jnp.concatenate([gathered[i], value], axis=0)
                    spread(i, depth - 1)
                else:
                    arrived[i, 0] = value
                    other[i] = swap(jnp.concatenate([gathered[i], value], axis=0), 0)
                    last[0] = value
            elif kind == "H":
                sums_of[i] = multiply([(mine[plans[i]][0], gated(gathered[i]))])
                last[0] = sums_of[i]
            elif kind == "M":
                if i in PLAIN:
                    sums_of[i] = sums_of[i] + dot(mine[plans[i]][1], gated(arrived[i, 0]))
                else:
                    sums_of[i] = multiply([(mine[plans[i]][1], gated(arrived[i, 0]))], sums_of[i])
                last[0] = sums_of[i]
                added.add(i)
            else:
                pairs = [] if i in added else [(mine[plans[i]][1], arrived[i, 0])]
                sides = gated(other[i]).reshape(2, -1, other[i].shape[1])
                pairs += [(theirs[plans[i]][side], sides[side]) for side in (0, 1)]
                if i in PLAIN:
                    sums_of[i] = sum((dot(*pair) for pair in pairs), sums_of[i]).astype(jnp.bfloat16)
                else:
                    sums_of[i] = multiply(pairs, sums_of[i], dtype=jnp.bfloat16)
                last[0] = sums_of[i]
        places = sorted((s, part.start, i) for i, (s, part) in enumerate(chunks))
        new_kv = jnp.concatenate([sums_of[i] for *_, i in places], axis=1)
        return (*outs, ratios, new_kv.reshape(-1, kinds, cols))

    return local


def solution(mesh):
    in_specs = (
        P("dp", None),
        P("dp", None, "tensor"),
        P("dp", None, "tensor"),
        P("dp", None, "tensor"),
        P("dp", None, "tensor"),
        P(),
    )
    out_specs = (
        P("dp", None, "tensor"),
        P("dp", None, "tensor"),
        P("dp", None, "tensor"),
        P(),
        P("dp", None, "tensor"),
    )
    local = make_local(mesh.shape["dp"], mesh.shape["tensor"])
    return jax.shard_map(local, mesh=mesh, in_specs=in_specs, out_specs=out_specs, check_vma=False)
```
